128 devices in a mesh: row: 16 (over x_lo, y, core), col: 8 (over z, x_hi).
Axes of the slice: x: 4 (x_hi: 2, x_lo: 2; x = x_hi * 2 + x_lo), y: 4, z: 4, core: 2. Of those that a mesh axis runs over, the one named last changes fastest.
Arguments:
- pair_elements: float32 [2, 1024, 20480], P(None, ('row', 'col')), may hold values from -24 to 24
- screened_w: float32 [20480, 20480], P('row', 'col'), may hold values from -0.0390625 to 0.0390625
- occupied: int32 [1024], P('row'), may hold values 0 or 1
- freq_index: int32 [1], replicated, may hold values from 0 to 15
Outputs:
- screened_pairs: float32 [2, 1024, 20480], P(None, 'row', 'col')
- sigma_bands: float32 [2, 1024], P(None, 'row')
The draws below stay inside these ranges and needn't reach their ends.
All inputs are finite; a program needn't handle non-finite values. No bound on the sum of `occupied` on one device may be relied on, other than what follows from the above.
Results may differ from the reference program's by a relative error of at most 0.000092.
Values sent between devices are 32-bit elements; how exact they have to be, the bound alone decides.
No kernel may reach another device: no remote copies, remote signals or barrier semaphores. Data moves between devices by JAX's collectives and lax.ppermute only.
A program may use at most 192 MiB of HBM per device.

```python
import jax
import jax.numpy as jnp
from jax import lax

NG = 20480
NFREQ = 16
NB = 1024


def with_ends(array, key, smallest, largest):
    index_at = [jax.random.randint(jax.random.fold_in(key, axis), (), 0, length) for axis, length in enumerate(array.shape)]
    longest = array.shape.index(max(array.shape))
    next_to = index_at[:longest] + [(index_at[longest] + 1) % array.shape[longest]] + index_at[longest + 1:]
    return array.at[tuple(index_at)].set(smallest).at[tuple(next_to)].set(largest)


def strengthened(array, rng, source, target, blocks, factor):
    owner, partner = [(jnp.arange(array.shape[position]) // (array.shape[position] // blocks)).reshape([-1 if axis == position else 1 for axis in range(array.ndim)]) for position in (source, target)]
    chosen = jax.random.permutation(rng, blocks)[partner]
    strong = (owner == chosen) | (owner == (partner + blocks // 2) % blocks)
    return jnp.where(strong, factor * array, array)


def steps_of(stream_key, extent, split, low, top_value):
    def one(dim, shards_of):
        draws = jax.random.uniform(jax.random.fold_in(jax.random.fold_in(stream_key, 6), dim), (shards_of,), jnp.float32, low / len(split), top_value / len(split))
        return jnp.repeat(jnp.exp(draws), extent[dim] // shards_of).reshape((-1,) + (1,) * (len(extent) - dim - 1))

    factor_of = one(*split[0])
    for cut in split[1:]:
        factor_of = factor_of * one(*cut)
    return factor_of


def noise(own_key, dims, scale, reach, split=(), held_as=jnp.bfloat16):
    drawn = jax.random.normal(own_key, dims, jnp.float32) * scale
    if len(split) > 0:
        drawn = steps_of(own_key, dims, split, -0.22, 0.18) * drawn
    return jnp.clip(drawn, min=-reach, max=reach).astype(held_as)


def noise_with(own_key, dims, spread, limit, cuts, heavy, kind=jnp.bfloat16):
    entries = spread * jax.random.normal(own_key, dims, jnp.float32)
    if cuts:
        entries = entries * steps_of(own_key, dims, cuts, -0.22, 0.18)
    return jnp.clip(strengthened(entries, jax.random.fold_in(own_key, 3), *heavy), -limit, limit).astype(kind)


def setup_inputs(seed: int = 0) -> dict:
    key_of = jax.random.split(jax.random.key(seed), 5)
    return {
        "pair_elements": noise_with(key_of[0], (2, NB, NG), 1.0, 24.0, ((1, 128),), (2, 1, 128, 5.5), jnp.float32),
        "screened_w": noise(key_of[1], (NG, NG), NG ** -0.5, 0.0390625, ((0, 16), (1, 8)), jnp.float32),
        "occupied": with_ends((jax.random.randint(key_of[2], (NB,), 0, 2) < 1).astype(jnp.int32), jax.random.fold_in(key_of[2], 1), 0, 1),
        "freq_index": jax.random.randint(key_of[3], (1,), 0, NFREQ).astype(jnp.int32),
    }


def reference(pair_elements, screened_w, occupied, freq_index):
    screened_pairs = jnp.einsum("kbg,gh->kbh", pair_elements, screened_w, precision=lax.Precision.HIGHEST, preferred_element_type=jnp.float32)
    real_part = jnp.sum(screened_pairs[0] * pair_elements[0] + screened_pairs[1] * pair_elements[1], axis=-1)
    imag_part = jnp.sum(screened_pairs[0] * pair_elements[1] - screened_pairs[1] * pair_elements[0], axis=-1)
    weight = 1.0 / (1.0 + 0.25 * freq_index[0].astype(jnp.float32))
    factor = weight * (0.5 - occupied.astype(jnp.float32)) * (NG ** -0.5)
    sigma_bands = jnp.stack([real_part * factor, imag_part * factor])
    return screened_pairs, sigma_bands
```

```python
import functools

import jax
import jax.numpy as jnp
from jax import lax
from jax.experimental import pallas as pl
from jax.experimental.pallas import tpu as pltpu
from jax.sharding import Mesh, PartitionSpec as P

NG = 20480
ROWS = 16
CHIP = 2560
HALF = 1280
TILE = 512
F32 = jnp.float32
BF16 = jnp.bfloat16

OWNERS = ((0, 2), (1, 1), (1, 2), (0, 3), (0, 1), (1, 3), (0, 0), (1, 0))
CHUNKS = ((0, 0), (0, 1), (1, 0), (3, 0), (1, 1), (3, 1), (2, 0), (2, 1))


def vmem():
    return pl.BlockSpec(memory_space=pltpu.VMEM)


def whole(shape):
    return jax.ShapeDtypeStruct(shape, F32)


def cut_kernel(place_ref, x_ref, *out_refs):
    for i in range(8):
        for part in range(2):
            start = pl.multiple_of(place_ref[2 * i + part], HALF)
            out_refs[i][:, part * HALF : (part + 1) * HALF] = x_ref[:, pl.ds(start, HALF)]
    for i in range(8):
        start = pl.multiple_of(place_ref[16 + i], CHIP)
        out_refs[8 + i][...] = x_ref[:, pl.ds(start, CHIP)]


def cut(place, x):
    return pl.pallas_call(
        cut_kernel,
        out_shape=[whole((ROWS, CHIP))] * 16,
        in_specs=[pl.BlockSpec(memory_space=pltpu.SMEM), vmem()],
        out_specs=[vmem()] * 16,
        compiler_params=pltpu.CompilerParams(vmem_limit_bytes=24 << 20),
        cost_estimate=pl.CostEstimate(flops=0, bytes_accessed=4 << 20, transcendentals=0),
    )(place, x)


def split(value):
    high = value.astype(BF16)
    return high, (value - high.astype(F32)).astype(BF16)


def screen_kernel(count, *refs):
    x_refs, (own_ref, other_ref) = refs[:count], refs[count : count + 2]
    outs, (both_ref,) = refs[count + 2 : -1], refs[-1:]
    rows = 128 * count

    @pl.when(pl.program_id(0) == 0)
    def _():
        for i in range(count):
            high, low = split(x_refs[i][...])
            both_ref[i * 128 : (i + 1) * 128, :] = high
            both_ref[rows + i * 128 : rows + (i + 1) * 128, :] = low

    total = jnp.zeros((rows, TILE), F32)
    for part, w_ref in enumerate((own_ref, other_ref)):
        at = slice(part * HALF, (part + 1) * HALF)
        high, low = split(w_ref[...])
        first = jnp.dot(both_ref[:, at], high, preferred_element_type=F32)
        total += first[:rows] + first[rows:]
        total += jnp.dot(both_ref[:rows, at], low, preferred_element_type=F32)
    for i in range(count):
        up, down, left = outs[3 * i : 3 * i + 3]
        base = i * 128
        up[...] = total[base : base + 32]
        down[...] = total[base + 32 : base + 64]
        left[...] = total[base + 64 : base + 128]


def screen(chunks, own, other):
    count = len(chunks)
    flops = 2 * 3 * 128 * count * CHIP * CHIP
    outs = pl.pallas_call(
        functools.partial(screen_kernel, count),
        grid=(CHIP // TILE,),
        out_shape=[whole((r, CHIP)) for _ in range(count) for r in (32, 32, 64)],
        in_specs=[pl.BlockSpec((128, CHIP), lambda i: (0, 0))] * count
        + [pl.BlockSpec((HALF, TILE), lambda i: (0, i))] * 2,
        out_specs=[
            pl.BlockSpec((r, TILE), lambda i: (0, i)) for _ in range(count) for r in (32, 32, 64)
        ],
        scratch_shapes=[pltpu.VMEM((256 * count, CHIP), BF16)],
        compiler_params=pltpu.CompilerParams(vmem_limit_bytes=56 << 20),
        cost_estimate=pl.CostEstimate(
            flops=flops, bytes_accessed=(30 + 3 * count) << 20, transcendentals=0
        ),
    )(*chunks, own, other)
    return [tuple(outs[3 * i : 3 * i + 3]) for i in range(count)]


def pass_kernel(left, up, down, to_up, to_down):
    to_up[...] = left[0:16, :] + up[0:16, :]
    to_down[...] = left[16:32, :] + down[0:16, :]


def turn_kernel(left, up, from_above, across):
    across[...] = left[48:64, :] + up[16:32, :] + from_above[...]


def small(kernel, outs, *args):
    return pl.pallas_call(
        kernel,
        out_shape=[whole((ROWS, CHIP))] * outs,
        in_specs=[vmem()] * len(args),
        out_specs=[vmem()] * outs,
        compiler_params=pltpu.CompilerParams(vmem_limit_bytes=16 << 20),
        cost_estimate=pl.CostEstimate(flops=0, bytes_accessed=1 << 20, transcendentals=0),
    )(*args)


def finish_kernel(place_ref, left, down, from_below, across, block, held, held_sums, out, sums):
    del place_ref, held, held_sums
    value = left[32:48, :] + down[16:32, :] + from_below[...] + across[...]
    out[0] = value[0:8]
    out[1] = value[8:16]
    real, imag = block[0:8, :], block[8:16, :]
    sums[0, 0:8, :] = jnp.sum(value[0:8] * real + value[8:16] * imag, axis=-1, keepdims=True)
    sums[0, 8:16, :] = jnp.sum(value[0:8] * imag - value[8:16] * real, axis=-1, keepdims=True)


def finish(place, left, down, from_below, across, block, held, held_sums):
    ins = (left, down, from_below, across, block)
    aliases, extra = {}, ()
    if held is not None:
        aliases, extra = {6: 0, 7: 1}, (held, held_sums)
        kernel = finish_kernel
    else:
        kernel = lambda p, *r: finish_kernel(p, *r[:5], None, None, *r[5:])
    return pl.pallas_call(
        kernel,
        grid_spec=pltpu.PrefetchScalarGridSpec(
            num_scalar_prefetch=1,
            grid=(1,),
            in_specs=[pl.BlockSpec(a.shape, lambda i, p: (0, 0)) for a in ins]
            + [pl.BlockSpec(memory_space=pl.ANY)] * len(extra),
            out_specs=[
                pl.BlockSpec((2, 8, CHIP), lambda i, p: (0, p[0], 0)),
                pl.BlockSpec((1, ROWS, 1), lambda i, p: (p[0], 0, 0)),
            ],
        ),
        out_shape=[whole((2, 64, CHIP)), whole((8, ROWS, 1))],
        input_output_aliases=aliases,
        compiler_params=pltpu.CompilerParams(vmem_limit_bytes=16 << 20),
        cost_estimate=pl.CostEstimate(flops=0, bytes_accessed=2 << 20, transcendentals=0),
    )(place, *ins, *extra)


def move(value, axis, by):
    size = {"xl": 2, "y": 4, "core": 2, "z": 4, "xh": 2}[axis]
    return lax.ppermute(value, axis, [(i, (i + by) % size) for i in range(size)])


def shift(value, axes, two, four):
    def at(a, b):
        return a * 4 + b if axes == ("xl", "y") else b * 2 + a

    pairs = [(at(a, b), at((a + two) % 2, (b + four) % 4)) for a in range(2) for b in range(4)]
    return lax.ppermute(value, axes, pairs)


def total_kernel(place_ref, factor, *refs):
    ins, out, held = refs[:8], refs[8], refs[9]
    for i in range(8):
        held[pl.ds(place_ref[i], 1)] = ins[i][...][None]
    out[...] = jnp.sum(held[...], axis=0) * factor[...]


def per_device(pair_elements, screened_w, occupied, freq_index):
    xl, y, core, z, xh = [lax.axis_index(a) for a in ("xl", "y", "core", "z", "xh")]
    other = move(screened_w, "core", 1)

    owner_places, col_places, chunk_places = [], [], []
    for dx, dy in OWNERS:
        block = ((xl + dx) % 2) * 4 + (y - dy) % 4
        owner_places += [block * CHIP + core * HALF, block * CHIP + (1 - core) * HALF]
    for dz, dx in CHUNKS:
        col_places.append((((z - dz) % 4) * 2 + (xh + dx) % 2) * CHIP)
        chunk_places.append(((z + dz) % 4) * 2 + (xh + dx) % 2)
    place = jnp.stack(owner_places + col_places).astype(jnp.int32)
    chunk_place = jnp.stack(chunk_places).astype(jnp.int32)
    pieces = cut(place, pair_elements.reshape(ROWS, NG))

    with jax.named_scope("rows_to_their_plane_waves"):
        rows = [
            p if d == (0, 0) else shift(p, ("xl", "y"), d[0], -d[1])
            for d, p in zip(OWNERS, pieces[:8])
        ]
        mine = jnp.concatenate(rows, axis=0)
    with jax.named_scope("second_index"):
        blocks = [
            p if d == (0, 0) else shift(p, ("z", "xh"), d[1], -d[0])
            for d, p in zip(CHUNKS, pieces[8:])
        ]

    with jax.named_scope("chunks"):
        chunk = {(0, 0): mine}
        chunk[0, 1] = move(mine, "xh", 1)
        chunk[3, 0] = move(mine, "z", 1)
        chunk[1, 0] = move(mine, "z", -1)
        chunk[1, 1] = move(chunk[1, 0], "xh", 1)
        chunk[3, 1] = move(chunk[0, 1], "z", 1)
        chunk[2, 0] = move(chunk[1, 0], "z", -1)
        chunk[2, 1] = jnp.concatenate(
            [move(chunk[3, 1][:64], "z", 1), move(chunk[1, 1][64:], "z", -1)], axis=0
        )

    out, sums = None, None
    for group in (((0, 0),), ((0, 1),), ((1, 0), (3, 0)), ((1, 1), (3, 1)), ((2, 0),), ((2, 1),)):
        terms = screen([chunk[c] for c in group], screened_w, other)
        for c, (up, down, left) in zip(group, terms):
            up, down = move(up, "y", 1), move(down, "y", -1)
            to_up, to_down = small(pass_kernel, 2, left, up, down)
            from_below, from_above = move(to_up, "y", 1), move(to_down, "y", -1)
            (across,) = small(turn_kernel, 1, left, up, from_above)
            across = move(across, "xl", 1)
            i = CHUNKS.index(c)
            out, sums = finish(
                chunk_place[i : i + 1], left, down, from_below, across, blocks[i], out, sums
            )

    with jax.named_scope("bands"):
        sums = sums.reshape(8, 2, 8).transpose(1, 0, 2).reshape(2, 64)
        everyone = [
            sums if d == (0, 0) else shift(sums, ("z", "xh"), d[1], -d[0]) for d in CHUNKS
        ]
        weight = 1.0 / (1.0 + 0.25 * freq_index[0].astype(F32))
        factor = weight * (0.5 - occupied.astype(F32)) * NG ** (-0.5)
        sigma = pl.pallas_call(
            total_kernel,
            out_shape=whole((2, 64)),
            in_specs=[pl.BlockSpec(memory_space=pltpu.SMEM)] + [vmem()] * 9,
            out_specs=vmem(),
            scratch_shapes=[pltpu.VMEM((8, 2, 64), F32)],
        )(chunk_place, factor.reshape(1, 64), *everyone)
    return out, sigma


def solution(mesh):
    fine = Mesh(mesh.devices.reshape(2, 4, 2, 4, 2), ("xl", "y", "core", "z", "xh"))
    row, col = ("xl", "y", "core"), ("z", "xh")
    return jax.shard_map(
        per_device,
        mesh=fine,
        in_specs=(P(None, row + col, None), P(row, col), P(row), P()),
        out_specs=(P(None, row, col), P(None, row)),
        check_vma=False,
    )
```

```python
import functools

import jax
import jax.numpy as jnp
from jax import lax
from jax.experimental import pallas as pl
from jax.experimental.pallas import tpu as pltpu
from jax.sharding import Mesh, PartitionSpec as P

NG = 20480
ROWS = 16
CHIP = 2560
HALF = 1280
TILE = 512
F32 = jnp.float32
BF16 = jnp.bfloat16
SIZES = {"xl": 2, "y": 4, "core": 2, "z": 4, "xh": 2}

OWNERS = ((0, 2), (1, 1), (1, 2), (0, 3), (0, 1), (1, 3), (0, 0), (1, 0))
WAVES = (((0, 0),), ((0, 1), (1, 0), (3, 0)), ((1, 1), (3, 1), (2, 0)), ((2, 1),))


def array(shape, dtype=F32):
    return jax.ShapeDtypeStruct(shape, dtype)


TOKEN = array((8, 128))
KEPT = pl.BlockSpec(memory_space=pltpu.HBM)
ANYWHERE = pl.BlockSpec(memory_space=pl.ANY)


def call(kernel, token, args, outs, in_specs, out_specs, grid, place=None, scratch=(), aliases=None, vmem=8):
    lead = 0 if place is None else 1
    n_in = lead + len(args)

    def body(*refs):
        rest = refs[n_in + 1 :]
        kernel(*refs[:n_in], *rest[: len(outs)], *rest[len(outs) + 1 :])

    result = pl.pallas_call(
        body,
        grid_spec=pltpu.PrefetchScalarGridSpec(
            num_scalar_prefetch=lead,
            grid=grid,
            in_specs=[*in_specs, ANYWHERE],
            out_specs=[*out_specs, ANYWHERE],
            scratch_shapes=list(scratch),
        ),
        out_shape=[*outs, TOKEN],
        input_output_aliases=aliases or {},
        compiler_params=pltpu.CompilerParams(vmem_limit_bytes=vmem << 20),
        cost_estimate=pl.CostEstimate(flops=1024, bytes_accessed=4096, transcendentals=0),
    )(*(() if place is None else (place,)), *args, token)
    return result[:-1], result[-1]


def tie(values, token):
    result = pl.pallas_call(
        lambda *refs: None,
        out_shape=[*(array(v.shape) for v in values), TOKEN],
        in_specs=[KEPT] * len(values) + [ANYWHERE],
        out_specs=[KEPT] * len(values) + [ANYWHERE],
        input_output_aliases={i: i for i in range(len(values))},
        cost_estimate=pl.CostEstimate(flops=1024, bytes_accessed=4096, transcendentals=0),
    )(*values, token)
    return result[:-1], result[-1]


def cut_kernel(place_ref, x_ref, by_row_ref, by_col_ref):
    core = place_ref[0]
    for i in range(8):
        start = pl.multiple_of(i * CHIP + core * HALF, HALF)
        by_row_ref[i, :, :HALF] = x_ref[:, pl.ds(start, HALF)]
        start = pl.multiple_of(i * CHIP + (1 - core) * HALF, HALF)
        by_row_ref[i, :, HALF:] = x_ref[:, pl.ds(start, HALF)]
        by_col_ref[i] = x_ref[:, i * CHIP : (i + 1) * CHIP]


def split(value):
    high = value.astype(BF16)
    return high, (value - high.astype(F32)).astype(BF16)


def halve(w, token):
    def kernel(w_ref, high_ref, low_ref):
        high_ref[0], low_ref[0] = split(w_ref[...])

    return call(
        kernel,
        token,
        [w],
        [array((CHIP // TILE, HALF, TILE), BF16)] * 2,
        [pl.BlockSpec((HALF, TILE), lambda i, *_: (0, i))],
        [pl.BlockSpec((1, HALF, TILE), lambda i, *_: (i, 0, 0))] * 2,
        (CHIP // TILE,),
        vmem=56,
    )


def screen_kernel(first, spare, sizes, place_ref, *refs):
    n_x = sum(sizes)
    x_refs, w_refs = refs[:n_x], refs[n_x : n_x + 3 + (not first)]
    up, down, left, *made, both_ref = refs[n_x + 3 + (not first) :]
    rows, n = 128 * len(sizes), ROWS * len(sizes)

    @pl.when(pl.program_id(0) == 0)
    def _():
        taken = 0
        for i, size in enumerate(sizes):
            for k in range(8):
                parts = [x_ref[place_ref[k]] for x_ref in x_refs[taken : taken + size]]
                high, low = split(parts[0] if size == 1 else jnp.concatenate(parts, axis=0))
                at = i * 128 + k * ROWS
                both_ref[at : at + ROWS, :] = high
                both_ref[rows + at : rows + at + ROWS, :] = low
            taken += size

    own_high, own_low, *other = w_refs
    if first:
        made[0][0], made[1][0] = split(other[0][...])
        other = made
    total = None
    for part, (high, low) in enumerate(((own_high, own_low), other)):
        at = slice(part * HALF, (part + 1) * HALF)
        product = jnp.dot(both_ref[:, at], high[0], preferred_element_type=F32)
        product = product[:rows] + product[rows:]
        product += jnp.dot(both_ref[:rows, at], low[0], preferred_element_type=F32)
        total = product if total is None else total + product
    for i in range(len(sizes)):
        for k, (ref, group) in enumerate(
            ((up, 0), (up, 1), (down, 0), (down, 1), (left, 0), (left, 1), (left, 2), (left, 3))
        ):
            at = (group + spare * (ref is not left)) * n + i * ROWS
            ref[at : at + ROWS, :] = total[i * 128 + k * ROWS : i * 128 + (k + 1) * ROWS]


def screen(owners, chunks, weights, token, spare=0):
    sizes = [len(c) for c in chunks]
    arrays = [a for c in chunks for a in c]
    n = ROWS * len(chunks)
    first = len(weights) == 3
    half = pl.BlockSpec((1, HALF, TILE), lambda i, *_: (i, 0, 0))
    return call(
        functools.partial(screen_kernel, first, spare, sizes),
        token,
        [*arrays, *weights],
        [array((k * n, CHIP)) for k in (2 + spare, 2 + spare, 4)] + [array((CHIP // TILE, HALF, TILE), BF16)] * (2 * first),
        [pl.BlockSpec(a.shape, lambda i, *_: (0, 0, 0)) for a in arrays]
        + [half] * 2
        + ([pl.BlockSpec((HALF, TILE), lambda i, *_: (0, i))] if first else [half] * 2),
        [pl.BlockSpec((k * n, TILE), lambda i, *_: (0, i)) for k in (2 + spare, 2 + spare, 4)] + [half] * (2 * first),
        (CHIP // TILE,),
        place=owners,
        scratch=[pltpu.VMEM((16 * n, CHIP), BF16)],
        vmem=56,
    )


def rows_at(n, *groups):
    tile = CHIP if n <= 16 else CHIP // 2
    return tile, [pl.BlockSpec((k * n, tile), lambda i, *_, at=at: (at, i)) for k, at in groups]


def pass_on(left, up, down, token, spare=0, into=()):
    n = left.shape[0] // 4

    def kernel(left, up, down, *rest):
        to_up, to_down = rest[-2:]
        to_up[...] = left[:n, :] + up[...]
        to_down[...] = left[n:, :] + down[...]

    tile, specs = rows_at(n, (2, 0), (1, spare), (1, spare), (1, 0), (1, 0))
    return call(
        kernel,
        token,
        [left, up, down, *into],
        [array((into[0] if into else up).shape) if into else array((n, CHIP))] * 2,
        specs[:3] + [KEPT] * len(into),
        specs[3:],
        (CHIP // tile,),
        aliases={3: 0, 4: 1} if into else {},
    )


def turn(left, up, down, below, above, token, spare=0):
    n = left.shape[0] // 4
    tile, specs = rows_at(n, (1, 2), (1, 3), (1, 1 + spare), (1, 1 + spare), (1, 0), (1, 0), (1, 0), (1, 0))

    def kernel(stay, go, up, down, below, above, kept, out):
        out[...] = go[...] + up[...] + above[...]
        kept[...] = stay[...] + down[...] + below[...]

    return call(
        kernel,
        token,
        [left, left, up, down, below, above],
        [array((n, CHIP))] * 2,
        specs[:6],
        specs[6:],
        (CHIP // tile,),
    )


def finish(place, kept, across, block, held, token):
    def kernel(place_ref, kept, across, block, *rest):
        out, sums = rest[-2:]
        value = kept[...] + across[...]
        out[0] = value[:8]
        out[1] = value[8:]
        real, imag = block[0, :8, :], block[0, 8:, :]
        sums[0, :8, :] = jnp.sum(value[:8] * real + value[8:] * imag, axis=-1, keepdims=True)
        sums[0, 8:, :] = jnp.sum(value[:8] * imag - value[8:] * real, axis=-1, keepdims=True)

    return call(
        kernel,
        token,
        [kept, across, block, *held],
        [array((2, 64, CHIP)), array((8, ROWS, 1))],
        [pl.BlockSpec((ROWS, CHIP), lambda i, p, k=k: (k + i, 0)) for k in (0, 0)]
        + [pl.BlockSpec((1, ROWS, CHIP), lambda i, p: (p[i], 0, 0))]
        + [KEPT] * len(held),
        [
            pl.BlockSpec((2, 8, CHIP), lambda i, p: (0, p[i], 0)),
            pl.BlockSpec((1, ROWS, 1), lambda i, p: (p[i], 0, 0)),
        ],
        (kept.shape[0] // ROWS,),
        place=place,
        aliases={4: 0, 5: 1} if held else {},
    )


def move(value, axis, by):
    size = SIZES[axis]
    return lax.ppermute(value, axis, [(i, (i + by) % size) for i in range(size)])


def per_device(pair_elements, screened_w, occupied, freq_index):
    xl, y, core, z, xh = [lax.axis_index(a) for a in SIZES]
    other = move(screened_w, "core", 1)
    owners = jnp.stack([(xl + a) % 2 * 4 + (y + b) % 4 for a, b in OWNERS]).astype(jnp.int32)
    places = jnp.stack([(z + a) % 4 * 2 + (xh + b) % 2 for w in WAVES for a, b in w]).astype(jnp.int32)
    weight = 1.0 / (1.0 + 0.25 * freq_index[0].astype(F32))
    factor = weight * (0.5 - occupied.astype(F32)) * NG ** (-0.5)

    token = jnp.zeros((8, 128), F32)
    whole3 = pl.BlockSpec((8, ROWS, CHIP), lambda i, *_: (0, 0, 0))
    (by_row, by_col), token = call(
        cut_kernel,
        token,
        [pair_elements.reshape(ROWS, NG)],
        [array((8, ROWS, CHIP))] * 2,
        [pl.BlockSpec((ROWS, NG), lambda i, *_: (0, 0))],
        [whole3] * 2,
        (1,),
        vmem=12,
        place=core.astype(jnp.int32).reshape(1),
    )
    with jax.named_scope("rows_to_their_plane_waves"):
        mine = lax.all_to_all(by_row, ("xl", "y"), 0, 0, tiled=True)
    halves, token = halve(screened_w, token)
    (mine,), token = tie([mine], token)
    chunk = {(0, 0): mine}
    with jax.named_scope("near_chunks"):
        chunk[0, 1] = move(mine, "xh", 1)
        chunk[3, 0] = move(mine, "z", 1)
        chunk[1, 0] = move(mine, "z", -1)

    (up0, down0, left0, *more), token = screen(owners, [[mine]], [*halves, other], token)
    halves = [*halves, *more]
    up0, down0 = move(up0, "y", 1), move(down0, "y", -1)
    (to_up, to_down), token = pass_on(left0, up0, down0, token)
    below0, above0 = move(to_up, "y", 1), move(to_down, "y", -1)

    with jax.named_scope("far_chunks"):
        got, token = tie([chunk[c] for c in WAVES[1]], token)
        chunk |= dict(zip(WAVES[1], got))
        chunk[1, 1] = move(chunk[1, 0], "xh", 1)
        chunk[3, 1] = move(chunk[0, 1], "z", 1)
        chunk[2, 0] = move(chunk[1, 0], "z", -1)

    (up1, down1, left1), token = screen(owners, [[chunk[c]] for c in WAVES[1]], halves, token)
    up1, down1 = move(up1, "y", 1), move(down1, "y", -1)
    (kept0, across0), token = turn(left0, up0, down0, below0, above0, token)
    across0 = move(across0, "xl", 1)

    with jax.named_scope("last_chunk"):
        got, token = tie([chunk[c] for c in WAVES[2]], token)
        chunk |= dict(zip(WAVES[2], got))
        last = [move(chunk[3, 1][:, :8], "z", 1), move(chunk[1, 1][:, 8:], "z", -1)]

    (up2, down2, left2), token = screen(owners, [[chunk[c]] for c in WAVES[2]], halves, token, 1)
    (up2, down2), token = pass_on(left1, up1, down1, token, 0, (up2, down2))
    up2, down2 = move(up2, "y", 1), move(down2, "y", -1)
    (*last, by_col), token = tie([*last, by_col], token)
    with jax.named_scope("second_index"):
        block = lax.all_to_all(by_col, ("z", "xh"), 0, 0, tiled=True)

    (up3, down3, left3), token = screen(owners, [last], halves, token)
    up3, down3 = move(up3, "y", 1), move(down3, "y", -1)

    held, token = finish(places[:1], kept0, across0, block, (), token)
    (to_up, to_down), token = pass_on(left2, up2, down2, token, 1)
    below2, above2 = move(to_up, "y", 1), move(to_down, "y", -1)
    (kept1, across1), token = turn(left1, up1, down1, up2, down2, token)
    across1 = move(across1, "xl", 1)
    (to_up, to_down), token = pass_on(left3, up3, down3, token)
    below3, above3 = move(to_up, "y", 1), move(to_down, "y", -1)
    (kept2, across2), token = turn(left2, up2, down2, below2, above2, token, 1)
    across2 = move(across2, "xl", 1)
    (kept3, across3), token = turn(left3, up3, down3, below3, above3, token)
    across3 = move(across3, "xl", 1)
    held, token = finish(places[1:4], kept1, across1, block, held, token)
    held, token = finish(places[4:7], kept2, across2, block, held, token)
    (out, sums), token = finish(places[7:], kept3, across3, block, held, token)

    with jax.named_scope("bands"):
        sums = sums.reshape(8, 2, 8).transpose(1, 0, 2).reshape(2, 64)
        sums = sums + move(sums, "xh", 1)
        for pairs in ([1, 0, 3, 2], [2, 3, 0, 1]):
            sums = sums + lax.ppermute(sums, "z", list(enumerate(pairs)))
    return out, sums * factor


def solution(mesh):
    fine = Mesh(mesh.devices.reshape(2, 4, 2, 4, 2), tuple(SIZES))
    row, col = ("xl", "y", "core"), ("z", "xh")
    return jax.shard_map(
        per_device,
        mesh=fine,
        in_specs=(P(None, row + col, None), P(row, col), P(row), P()),
        out_specs=(P(None, row, col), P(None, row)),
        check_vma=False,
    )
```

```python
import functools

import jax
import jax.numpy as jnp
from jax import lax
from jax.experimental import pallas as pl
from jax.experimental.pallas import tpu as pltpu
from jax.sharding import Mesh, PartitionSpec as P

NG = 20480
ROWS = 16
CHIP = 2560
HALF = 1280
TILE = 512
F32 = jnp.float32
BF16 = jnp.bfloat16
SIZES = {"xl": 2, "y": 4, "core": 2, "z": 4, "xh": 2}

OWNERS = ((0, 2), (1, 1), (1, 2), (0, 3), (0, 1), (1, 3), (0, 0), (1, 0))
WAVES = (((0, 0),), ((0, 1), (1, 0), (3, 0)), ((1, 1), (3, 1)), ((2, 0), (2, 1)))


def array(shape, dtype=F32):
    return jax.ShapeDtypeStruct(shape, dtype)


TOKEN = array((6656, CHIP))


def in_hbm(value):
    if isinstance(value, jax.ShapeDtypeStruct):
        return pltpu.HBM(value.shape, value.dtype)
    return pltpu.with_memory_space_constraint(value, pltpu.HBM)


KEPT = pl.BlockSpec(memory_space=pltpu.HBM)


def call(kernel, token, args, outs, in_specs, out_specs, grid, place=None, scratch=(), aliases=None, vmem=8):
    lead = 0 if place is None else 1
    n_in = lead + len(args)
    before = () if token is None else (token,)

    def body(*refs):
        rest = refs[n_in + len(before) :]
        kernel(*refs[:n_in], *rest[: len(outs)], *rest[len(outs) + 1 :])

    result = pl.pallas_call(
        body,
        grid_spec=pltpu.PrefetchScalarGridSpec(
            num_scalar_prefetch=lead,
            grid=grid,
            in_specs=[*in_specs, *(KEPT for _ in before)],
            out_specs=[*out_specs, KEPT],
            scratch_shapes=list(scratch),
        ),
        out_shape=[*outs, TOKEN],
        input_output_aliases=(aliases or {}) | ({n_in: len(outs)} if before else {}),
        compiler_params=pltpu.CompilerParams(vmem_limit_bytes=vmem << 20),
        cost_estimate=pl.CostEstimate(flops=1024, bytes_accessed=4096, transcendentals=0),
    )(*(() if place is None else (place,)), *args, *before)
    return result[:-1], result[-1]


def tie(values, token, space=pltpu.VMEM):
    n = len(values) + 1
    outs = [array(v.shape) for v in values]
    if space is pltpu.HBM:
        values, outs = [in_hbm(v) for v in values], [in_hbm(o) for o in outs]
    specs = [pl.BlockSpec(memory_space=space)] * len(values) + [KEPT]
    result = pl.pallas_call(
        lambda *refs: None,
        out_shape=[*outs, TOKEN],
        in_specs=specs,
        out_specs=specs,
        input_output_aliases={i: i for i in range(n)},
        compiler_params=pltpu.CompilerParams(vmem_limit_bytes=16 << 20),
        cost_estimate=pl.CostEstimate(flops=1024, bytes_accessed=4096, transcendentals=0),
    )(*values, token)
    return result[:-1], result[-1]


def cut_kernel(place_ref, x_ref, by_row_ref, by_col_ref):
    core = place_ref[0]
    for i in range(8):
        start = pl.multiple_of(i * CHIP + core * HALF, HALF)
        by_row_ref[i, :, :HALF] = x_ref[:, pl.ds(start, HALF)]
        start = pl.multiple_of(i * CHIP + (1 - core) * HALF, HALF)
        by_row_ref[i, :, HALF:] = x_ref[:, pl.ds(start, HALF)]
        by_col_ref[i] = x_ref[:, i * CHIP : (i + 1) * CHIP]


def split(value):
    high = value.astype(BF16)
    return high, (value - high.astype(F32)).astype(BF16)


def halve(w, token):
    def kernel(w_ref, halves_ref):
        halves_ref[0, 0], halves_ref[1, 0] = split(w_ref[...])

    return call(
        kernel,
        token,
        [w],
        [array((4, CHIP // TILE, HALF, TILE), BF16)],
        [pl.BlockSpec((HALF, TILE), lambda i, *_: (0, i))],
        [pl.BlockSpec((2, 1, HALF, TILE), lambda i, *_: (0, i, 0, 0))],
        (CHIP // TILE,),
        vmem=40,
    )


def screen_kernel(first, sizes, place_ref, *refs):
    n_x = sum(sizes)
    x_refs, halves_ref, rest = refs[:n_x], refs[n_x], refs[n_x + 1 :]
    up, down, left, *made, both_ref = rest[1:] if first else rest
    rows, n = 128 * len(sizes), ROWS * len(sizes)

    @pl.when(pl.program_id(0) == 0)
    def _():
        taken = 0
        for i, size in enumerate(sizes):
            for k in range(8):
                parts = [x_ref[place_ref[k]] for x_ref in x_refs[taken : taken + size]]
                high, low = split(parts[0] if size == 1 else jnp.concatenate(parts, axis=0))
                at = i * 128 + k * ROWS
                both_ref[at : at + ROWS, :] = high
                both_ref[rows + at : rows + at + ROWS, :] = low
            taken += size

    weights = [halves_ref[k, 0] for k in range(2 if first else 4)]
    if first:
        made[0][0, 0], made[0][1, 0] = split(rest[0][...])
        weights += [made[0][0, 0], made[0][1, 0]]
    total = None
    for part in range(2):
        high, low = weights[2 * part : 2 * part + 2]
        at = slice(part * HALF, (part + 1) * HALF)
        product = jnp.dot(both_ref[:, at], high, preferred_element_type=F32)
        product = product[:rows] + product[rows:]
        product += jnp.dot(both_ref[:rows, at], low, preferred_element_type=F32)
        total = product if total is None else total + product
    for i in range(len(sizes)):
        for k, (ref, group) in enumerate(
            ((up, 0), (up, 1), (down, 0), (down, 1), (left, 0), (left, 1), (left, 2), (left, 3))
        ):
            at = group * n + i * ROWS
            ref[at : at + ROWS, :] = total[i * 128 + k * ROWS : i * 128 + (k + 1) * ROWS]


def screen(owners, chunks, weights, token, spare=0):
    sizes = [len(c) for c in chunks]
    arrays = [a for c in chunks for a in c]
    n = ROWS * len(chunks)
    rows = (2 * n + spare, 2 * n + spare, 4 * n)
    first = len(weights) == 2
    halves = [pl.BlockSpec((k, 1, HALF, TILE), lambda i, *_, at=at: (at, i, 0, 0)) for k, at in ((4, 0), (2, 0), (2, 1))]
    return call(
        functools.partial(screen_kernel, first, sizes),
        token,
        [*arrays, *weights],
        [array((r, CHIP)) for r in rows[:2]] + [in_hbm(array((rows[2], CHIP)))] + [array(weights[0].shape, BF16)] * first,
        [pl.BlockSpec(a.shape, lambda i, *_: (0, 0, 0)) for a in arrays]
        + ([halves[1], pl.BlockSpec((HALF, TILE), lambda i, *_: (0, i))] if first else [halves[0]]),
        [pl.BlockSpec((r, TILE), lambda i, *_: (0, i)) for r in rows] + [halves[2]] * first,
        (CHIP // TILE,),
        place=owners,
        scratch=[pltpu.VMEM((16 * n, CHIP), BF16)],
        aliases={1 + len(arrays): 3} if first else {},
        vmem=40,
    )


def rows_from(*firsts):
    return [pl.BlockSpec((ROWS, CHIP), lambda i, *_, at=at // ROWS: (at + i, 0)) for at in firsts]


def pass_on(left, up, down, token, into=()):
    n = left.shape[0] // 4
    outs = [array(a.shape) for a in into] or [array((n, CHIP))] * 2

    def kernel(left_up, left_down, up, down, *rest):
        to_up, to_down = rest[-2:]
        to_up[...] = left_up[...] + up[...]
        to_down[...] = left_down[...] + down[...]

    return call(
        kernel,
        token,
        [in_hbm(left), in_hbm(left), up, down, *into],
        outs,
        rows_from(0, n, 0, 0) + [KEPT] * len(into),
        rows_from(outs[0].shape[0] - n, outs[0].shape[0] - n),
        (n // ROWS,),
        aliases={4: 0, 5: 1} if into else {},
    )


def turn(left, up, down, below, above, token, spare=0, into=()):
    n = left.shape[0] // 4
    passed = below.shape[0] - n
    outs = [array(a.shape) for a in into] or [array((n + spare, CHIP))] * 2
    at = outs[0].shape[0] - n if into else 0

    def kernel(stay, go, up, down, below, above, *rest):
        kept, out = rest[-2:]
        out[...] = go[...] + up[...] + above[...]
        kept[...] = stay[...] + down[...] + below[...]

    return call(
        kernel,
        token,
        [in_hbm(left), in_hbm(left), up, down, below, above, *into],
        [in_hbm(outs[0]), outs[1]],
        rows_from(2 * n, 3 * n, n, n, passed, passed) + [KEPT] * len(into),
        rows_from(at, at),
        (n // ROWS,),
        aliases={6: 0, 7: 1} if into else {},
    )


def finish(place, kept, across, block, held, token):
    def kernel(place_ref, kept, across, block, *rest):
        out, sums = rest[-2:]
        value = kept[...] + across[...]
        out[0] = value[:8]
        out[1] = value[8:]
        real, imag = block[0, :8, :], block[0, 8:, :]
        sums[0, :8, :] = jnp.sum(value[:8] * real + value[8:] * imag, axis=-1, keepdims=True)
        sums[0, 8:, :] = jnp.sum(value[:8] * imag - value[8:] * real, axis=-1, keepdims=True)

    return call(
        kernel,
        token,
        [in_hbm(kept), across, block, *held],
        [array((2, 64, CHIP)), array((8, ROWS, 1))],
        [pl.BlockSpec((ROWS, CHIP), lambda i, p, k=k: (k + i, 0)) for k in (0, 0)]
        + [pl.BlockSpec((1, ROWS, CHIP), lambda i, p: (p[i], 0, 0))]
        + [KEPT] * len(held),
        [
            pl.BlockSpec((2, 8, CHIP), lambda i, p: (0, p[i], 0)),
            pl.BlockSpec((1, ROWS, 1), lambda i, p: (p[i], 0, 0)),
        ],
        (kept.shape[0] // ROWS,),
        place=place,
        aliases={4: 0, 5: 1} if held else {},
    )


def move(value, axis, by):
    size = SIZES[axis]
    return lax.ppermute(value, axis, [(i, (i + by) % size) for i in range(size)])


def per_device(pair_elements, screened_w, occupied, freq_index):
    xl, y, core, z, xh = [lax.axis_index(a) for a in SIZES]
    other = move(screened_w, "core", 1)
    owners = jnp.stack([(xl + a) % 2 * 4 + (y + b) % 4 for a, b in OWNERS]).astype(jnp.int32)
    places = jnp.stack([(z + a) % 4 * 2 + (xh + b) % 2 for w in WAVES for a, b in w]).astype(jnp.int32)
    weight = 1.0 / (1.0 + 0.25 * freq_index[0].astype(F32))
    factor = weight * (0.5 - occupied.astype(F32)) * NG ** (-0.5)

    whole3 = pl.BlockSpec((8, ROWS, CHIP), lambda i, *_: (0, 0, 0))
    (by_row, by_col), token = call(
        cut_kernel,
        None,
        [in_hbm(pair_elements.reshape(ROWS, NG))],
        [in_hbm(array((8, ROWS, CHIP)))] * 2,
        [pl.BlockSpec((ROWS, NG), lambda i, *_: (0, 0))],
        [whole3] * 2,
        (1,),
        vmem=12,
        place=core.astype(jnp.int32).reshape(1),
    )
    with jax.named_scope("rows_to_their_plane_waves"):
        mine = lax.all_to_all(by_row, ("xl", "y"), 0, 0, tiled=True)
    halves, token = halve(screened_w, token)
    (mine,), token = tie([mine], token)
    chunk = {(0, 0): mine}
    with jax.named_scope("near_chunks"):
        chunk[3, 0] = move(mine, "z", 1)
        chunk[1, 0] = move(mine, "z", -1)
        chunk[0, 1] = move(mine, "xh", 1)

    (up0, down0, left0, *halves), token = screen(owners, [[mine]], [*halves, other], token)
    up0, down0 = move(up0, "y", 1), move(down0, "y", -1)

    with jax.named_scope("far_chunks"):
        (up0, down0), token = tie([up0, down0], token, pl.ANY)
        got, token = tie([chunk[c] for c in WAVES[1]], token, pl.ANY)
        chunk |= dict(zip(WAVES[1], got))
        chunk[3, 1] = move(chunk[0, 1], "z", 1)
        chunk[2, 0] = move(chunk[1, 0], "z", -1)
        chunk[1, 1] = move(chunk[1, 0], "xh", 1)

    (up1, down1, left1), token = screen(owners, [[in_hbm(chunk[c])] for c in WAVES[1]], halves, token, ROWS)
    (up1, down1), token = pass_on(left0, up0, down0, token, (up1, down1))
    up1, down1 = move(up1, "y", 1), move(down1, "y", -1)

    with jax.named_scope("last_chunk"):
        later = (*WAVES[2], (2, 0))
        got, token = tie([chunk[c] for c in later], token)
        chunk |= dict(zip(later, got))
        last = [move(chunk[3, 1][:, :8], "z", 1), move(chunk[1, 1][:, 8:], "z", -1)]

    (up2, down2, left2), token = screen(owners, [[chunk[c]] for c in WAVES[2]], halves, token, 3 * ROWS)
    last, token = tie(last, token)
    (by_col,), token = tie([by_col], token, pltpu.HBM)
    with jax.named_scope("second_index"):
        block = lax.all_to_all(by_col, ("z", "xh"), 0, 0, tiled=True)
    (up2, down2), token = pass_on(left1, up1, down1, token, (up2, down2))
    up2, down2 = move(up2, "y", 1), move(down2, "y", -1)
    begun, token = turn(left0, up0, down0, up1, down1, token, 3 * ROWS)

    (up3, down3, left3), token = screen(owners, [[chunk[2, 0]], last], halves, token)
    up3, down3 = move(up3, "y", 1), move(down3, "y", -1)
    (block,), token = tie([block], token, pltpu.HBM)
    (kept1, across1), token = turn(left1, up1, down1, up2, down2, token, 0, begun)
    across1 = move(across1, "xl", 1)
    (to_up, to_down), token = pass_on(left2, up2, down2, token)
    below2, above2 = move(to_up, "y", 1), move(to_down, "y", -1)
    (to_up, to_down), token = pass_on(left3, up3, down3, token)
    below3, above3 = move(to_up, "y", 1), move(to_down, "y", -1)
    (kept2, across2), token = turn(left2, up2, down2, below2, above2, token)
    across2 = move(across2, "xl", 1)
    (across1,), token = tie([across1], token)
    (kept3, across3), token = turn(left3, up3, down3, below3, above3, token)
    across3 = move(across3, "xl", 1)
    held, token = finish(places[:4], kept1, across1, block, (), token)
    held, token = finish(places[4:6], kept2, across2, block, held, token)
    (out, sums), token = finish(places[6:], kept3, across3, block, held, token)

    with jax.named_scope("bands"):
        sums = sums.reshape(8, 2, 8).transpose(1, 0, 2).reshape(2, 64)
        sums = sums + move(sums, "xh", 1)
        sums = (sums + move(sums, "z", 2)) + (move(sums, "z", 1) + move(sums, "z", -1))
    return out, sums * factor


def solution(mesh):
    fine = Mesh(mesh.devices.reshape(2, 4, 2, 4, 2), tuple(SIZES))
    row, col = ("xl", "y", "core"), ("z", "xh")
    return jax.shard_map(
        per_device,
        mesh=fine,
        in_specs=(P(None, row + col, None), P(row, col), P(row), P()),
        out_specs=(P(None, row, col), P(None, row)),
        check_vma=False,
    )
```

```python
import functools

import jax
import jax.numpy as jnp
from jax import lax
from jax.experimental import pallas as pl
from jax.experimental.pallas import tpu as pltpu
from jax.sharding import Mesh, PartitionSpec as P

NG = 20480
ROWS = 16
CHIP = 2560
HALF = 1280
TILE = 512
F32 = jnp.float32
BF16 = jnp.bfloat16
SIZES = {"xl": 2, "y": 4, "core": 2, "z": 4, "xh": 2}

OWNERS = ((0, 2), (1, 1), (1, 2), (0, 3), (0, 1), (1, 3), (0, 0), (1, 0))
WAVES = (((0, 0),), ((0, 1), (1, 0), (3, 0)), ((1, 1), (3, 1)), ((2, 0), (2, 1)))


def array(shape, dtype=F32):
    return jax.ShapeDtypeStruct(shape, dtype)


TOKEN = array((6656, CHIP))


def in_hbm(value):
    if isinstance(value, jax.ShapeDtypeStruct):
        return pltpu.HBM(value.shape, value.dtype)
    return pltpu.with_memory_space_constraint(value, pltpu.HBM)


KEPT = pl.BlockSpec(memory_space=pltpu.HBM)


def call(kernel, token, args, outs, in_specs, out_specs, grid, place=None, scratch=(), aliases=None, vmem=8):
    lead = 0 if place is None else 1
    n_in = lead + len(args)
    before = () if token is None else (token,)

    def body(*refs):
        rest = refs[n_in + len(before) :]
        kernel(*refs[:n_in], *rest[: len(outs)], *rest[len(outs) + 1 :])

    result = pl.pallas_call(
        body,
        grid_spec=pltpu.PrefetchScalarGridSpec(
            num_scalar_prefetch=lead,
            grid=grid,
            in_specs=[*in_specs, *(KEPT for _ in before)],
            out_specs=[*out_specs, KEPT],
            scratch_shapes=list(scratch),
        ),
        out_shape=[*outs, TOKEN],
        input_output_aliases=(aliases or {}) | ({n_in: len(outs)} if before else {}),
        compiler_params=pltpu.CompilerParams(vmem_limit_bytes=vmem << 20),
        cost_estimate=pl.CostEstimate(flops=1024, bytes_accessed=4096, transcendentals=0),
    )(*(() if place is None else (place,)), *args, *before)
    return result[:-1], result[-1]


def tie(values, token, space=pltpu.VMEM):
    n = len(values) + 1
    outs = [array(v.shape) for v in values]
    if space is pltpu.HBM:
        values, outs = [in_hbm(v) for v in values], [in_hbm(o) for o in outs]
    specs = [pl.BlockSpec(memory_space=space)] * len(values) + [KEPT]
    result = pl.pallas_call(
        lambda *refs: None,
        out_shape=[*outs, TOKEN],
        in_specs=specs,
        out_specs=specs,
        input_output_aliases={i: i for i in range(n)},
        compiler_params=pltpu.CompilerParams(vmem_limit_bytes=16 << 20),
        cost_estimate=pl.CostEstimate(flops=1024, bytes_accessed=4096, transcendentals=0),
    )(*values, token)
    return result[:-1], result[-1]


def cut_kernel(place_ref, x_ref, by_row_ref, by_col_ref):
    core = place_ref[0]
    for i in range(8):
        start = pl.multiple_of(i * CHIP + core * HALF, HALF)
        by_row_ref[i, :, :HALF] = x_ref[:, pl.ds(start, HALF)]
        start = pl.multiple_of(i * CHIP + (1 - core) * HALF, HALF)
        by_row_ref[i, :, HALF:] = x_ref[:, pl.ds(start, HALF)]
        by_col_ref[i] = x_ref[:, i * CHIP : (i + 1) * CHIP]


def split(value):
    high = value.astype(BF16)
    return high, (value - high.astype(F32)).astype(BF16)


def halve(w, token):
    def kernel(w_ref, halves_ref):
        halves_ref[0, 0], halves_ref[1, 0] = split(w_ref[...])

    return call(
        kernel,
        token,
        [w],
        [array((4, CHIP // TILE, HALF, TILE), BF16)],
        [pl.BlockSpec((HALF, TILE), lambda i, *_: (0, i))],
        [pl.BlockSpec((2, 1, HALF, TILE), lambda i, *_: (0, i, 0, 0))],
        (CHIP // TILE,),
        vmem=40,
    )


def screen_kernel(first, sizes, beside, n_beside, place_ref, *refs):
    n_x = sum(sizes)
    x_refs, halves_ref, rest = refs[:n_x], refs[n_x], refs[n_x + 1 :]
    *rest, both_ref = rest
    beside_refs, (up, down, left, *made) = rest[first : first + n_beside], rest[first + n_beside :]
    rows, n = 128 * len(sizes), ROWS * len(sizes)

    @pl.when(pl.program_id(0) == 0)
    def _():
        taken = 0
        for i, size in enumerate(sizes):
            for k in range(8):
                parts = [x_ref[place_ref[k]] for x_ref in x_refs[taken : taken + size]]
                high, low = split(parts[0] if size == 1 else jnp.concatenate(parts, axis=0))
                at = i * 128 + k * ROWS
                both_ref[at : at + ROWS, :] = high
                both_ref[rows + at : rows + at + ROWS, :] = low
            taken += size

    weights = [halves_ref[k, 0] for k in range(2 if first else 4)]
    if first:
        made[0][0, 0], made[0][1, 0] = split(rest[0][...])
        weights += [made[0][0, 0], made[0][1, 0]]
    total = None
    for part in range(2):
        high, low = weights[2 * part : 2 * part + 2]
        at = slice(part * HALF, (part + 1) * HALF)
        product = jnp.dot(both_ref[:, at], high, preferred_element_type=F32)
        product = product[:rows] + product[rows:]
        product += jnp.dot(both_ref[:rows, at], low, preferred_element_type=F32)
        total = product if total is None else total + product
    if beside is not None:
        beside(beside_refs, up, down, made)
    for i in range(len(sizes)):
        for k, (ref, group) in enumerate(
            ((up, 0), (up, 1), (down, 0), (down, 1), (left, 0), (left, 1), (left, 2), (left, 3))
        ):
            at = group * n + i * ROWS
            ref[at : at + ROWS, :] = total[i * 128 + k * ROWS : i * 128 + (k + 1) * ROWS]


def screen(owners, chunks, weights, token, spare=0, beside=None, beside_args=(), beside_specs=(), more=()):
    sizes = [len(c) for c in chunks]
    arrays = [a for c in chunks for a in c]
    n = ROWS * len(chunks)
    rows = (2 * n + spare, 2 * n + spare, 4 * n)
    first = len(weights) == 2
    halves = [pl.BlockSpec((k, 1, HALF, TILE), lambda i, *_, at=at: (at, i, 0, 0)) for k, at in ((4, 0), (2, 0), (2, 1))]
    return call(
        functools.partial(screen_kernel, first, sizes, beside, len(beside_args)),
        token,
        [*arrays, *weights, *beside_args],
        [array((r, CHIP)) for r in rows[:2]]
        + [in_hbm(array((rows[2], CHIP)))]
        + [array(weights[0].shape, BF16)] * first
        + [*more],
        [pl.BlockSpec(a.shape, lambda i, *_: (0, 0, 0)) for a in arrays]
        + ([halves[1], pl.BlockSpec((HALF, TILE), lambda i, *_: (0, i))] if first else [halves[0]])
        + [*beside_specs],
        [pl.BlockSpec((r, TILE), lambda i, *_: (0, i)) for r in rows]
        + [halves[2]] * first
        + [pl.BlockSpec((m.shape[0], TILE), lambda i, *_: (0, i)) for m in more],
        (CHIP // TILE,),
        place=owners,
        scratch=[pltpu.VMEM((16 * n, CHIP), BF16)],
        aliases={1 + len(arrays): 3} if first else {},
        vmem=40,
    )


def tiles_from(*firsts):
    return [pl.BlockSpec((ROWS, TILE), lambda i, *_, at=at // ROWS: (at, i)) for at in firsts]


def pass_beside(refs, up, down, made):
    left_up, left_down, from_up, from_down = refs
    up[-ROWS:, :] = left_up[...] + from_up[...]
    down[-ROWS:, :] = left_down[...] + from_down[...]


def turn_beside(refs, up, down, made):
    stay, go, from_up, from_down, below, above = refs
    kept, out = made
    kept[:ROWS, :] = stay[...] + from_down[...] + below[...]
    out[:ROWS, :] = go[...] + from_up[...] + above[...]


def rows_from(*firsts):
    return [pl.BlockSpec((ROWS, CHIP), lambda i, *_, at=at // ROWS: (at + i, 0)) for at in firsts]


def pass_on(left, up, down, token, into=()):
    n = left.shape[0] // 4
    outs = [array(a.shape) for a in into] or [array((n, CHIP))] * 2

    def kernel(left_up, left_down, up, down, *rest):
        to_up, to_down = rest[-2:]
        to_up[...] = left_up[...] + up[...]
        to_down[...] = left_down[...] + down[...]

    return call(
        kernel,
        token,
        [in_hbm(left), in_hbm(left), up, down, *into],
        outs,
        rows_from(0, n, 0, 0) + [KEPT] * len(into),
        rows_from(outs[0].shape[0] - n, outs[0].shape[0] - n),
        (n // ROWS,),
        aliases={4: 0, 5: 1} if into else {},
    )


def turn(left, up, down, below, above, token, spare=0, into=(), keep=in_hbm):
    n = left.shape[0] // 4
    passed = below.shape[0] - n
    outs = [array(a.shape) for a in into] or [array((n + spare, CHIP))] * 2
    at = outs[0].shape[0] - n if into else 0

    def kernel(stay, go, up, down, below, above, *rest):
        kept, out = rest[-2:]
        out[...] = go[...] + up[...] + above[...]
        kept[...] = stay[...] + down[...] + below[...]

    return call(
        kernel,
        token,
        [in_hbm(left), in_hbm(left), up, down, below, above, *into],
        [keep(outs[0]), outs[1]],
        rows_from(2 * n, 3 * n, n, n, passed, passed) + [KEPT] * len(into),
        rows_from(at, at),
        (n // ROWS,),
        aliases={6: 0, 7: 1} if into else {},
    )


def finish(place, kept, across, block, held, token, keep=in_hbm):
    def kernel(place_ref, kept, across, block, *rest):
        out, sums = rest[-2:]
        value = kept[...] + across[...]
        out[0] = value[:8]
        out[1] = value[8:]
        real, imag = block[0, :8, :], block[0, 8:, :]
        sums[0, :8, :] = jnp.sum(value[:8] * real + value[8:] * imag, axis=-1, keepdims=True)
        sums[0, 8:, :] = jnp.sum(value[:8] * imag - value[8:] * real, axis=-1, keepdims=True)

    return call(
        kernel,
        token,
        [keep(kept), across, block, *held],
        [array((2, 64, CHIP)), array((8, ROWS, 1))],
        [pl.BlockSpec((ROWS, CHIP), lambda i, p, k=k: (k + i, 0)) for k in (0, 0)]
        + [pl.BlockSpec((1, ROWS, CHIP), lambda i, p: (p[i], 0, 0))]
        + [KEPT] * len(held),
        [
            pl.BlockSpec((2, 8, CHIP), lambda i, p: (0, p[i], 0)),
            pl.BlockSpec((1, ROWS, 1), lambda i, p: (p[i], 0, 0)),
        ],
        (kept.shape[0] // ROWS,),
        place=place,
        aliases={4: 0, 5: 1} if held else {},
    )


def move(value, axis, by):
    size = SIZES[axis]
    return lax.ppermute(value, axis, [(i, (i + by) % size) for i in range(size)])


def per_device(pair_elements, screened_w, occupied, freq_index):
    xl, y, core, z, xh = [lax.axis_index(a) for a in SIZES]
    other = move(screened_w, "core", 1)
    owners = jnp.stack([(xl + a) % 2 * 4 + (y + b) % 4 for a, b in OWNERS]).astype(jnp.int32)
    places = jnp.stack([(z + a) % 4 * 2 + (xh + b) % 2 for w in WAVES for a, b in w]).astype(jnp.int32)
    weight = 1.0 / (1.0 + 0.25 * freq_index[0].astype(F32))
    factor = weight * (0.5 - occupied.astype(F32)) * NG ** (-0.5)

    whole3 = pl.BlockSpec((8, ROWS, CHIP), lambda i, *_: (0, 0, 0))
    (by_row, by_col), token = call(
        cut_kernel,
        None,
        [in_hbm(pair_elements.reshape(ROWS, NG))],
        [in_hbm(array((8, ROWS, CHIP)))] * 2,
        [pl.BlockSpec((ROWS, NG), lambda i, *_: (0, 0))],
        [whole3] * 2,
        (1,),
        vmem=12,
        place=core.astype(jnp.int32).reshape(1),
    )
    with jax.named_scope("rows_to_their_plane_waves"):
        mine = lax.all_to_all(by_row, ("xl", "y"), 0, 0, tiled=True)
    halves, token = halve(screened_w, token)
    (mine,), token = tie([mine], token)
    chunk = {(0, 0): mine}
    with jax.named_scope("near_chunks"):
        chunk[3, 0] = move(mine, "z", 1)
        chunk[1, 0] = move(mine, "z", -1)
        chunk[0, 1] = move(mine, "xh", 1)

    (up0, down0, left0, *halves), token = screen(owners, [[mine]], [*halves, other], token)
    up0, down0 = move(up0, "y", 1), move(down0, "y", -1)

    with jax.named_scope("far_chunks"):
        (up0, down0), token = tie([up0, down0], token, pl.ANY)
        got, token = tie([chunk[c] for c in WAVES[1]], token, pl.ANY)
        chunk |= dict(zip(WAVES[1], got))
        chunk[3, 1] = move(chunk[0, 1], "z", 1)
        chunk[2, 0] = move(chunk[1, 0], "z", -1)
        chunk[1, 1] = move(chunk[1, 0], "xh", 1)

    (up1, down1, left1), token = screen(
        owners,
        [[in_hbm(chunk[0, 1])], [in_hbm(chunk[1, 0])], [chunk[3, 0]]],
        halves,
        token,
        ROWS,
        pass_beside,
        [in_hbm(left0), in_hbm(left0), up0, down0],
        tiles_from(0, ROWS, 0, 0),
    )
    up1, down1 = move(up1, "y", 1), move(down1, "y", -1)

    with jax.named_scope("last_chunk"):
        later = (*WAVES[2], (2, 0))
        got, token = tie([chunk[c] for c in later], token)
        chunk |= dict(zip(later, got))
        last = [move(chunk[3, 1][:, :8], "z", 1), move(chunk[1, 1][:, 8:], "z", -1)]

    (up2, down2, left2), token = screen(owners, [[chunk[c]] for c in WAVES[2]], halves, token, 3 * ROWS)
    last, token = tie(last, token)
    (up2, down2), token = pass_on(left1, up1, down1, token, (up2, down2))
    up2, down2 = move(up2, "y", 1), move(down2, "y", -1)

    (by_col,), token = tie([by_col], token, pltpu.HBM)
    with jax.named_scope("second_index"):
        block = lax.all_to_all(by_col, ("z", "xh"), 0, 0, tiled=True)
    (up3, down3, left3, *begun), token = screen(
        owners,
        [[in_hbm(chunk[2, 0])], [in_hbm(a) for a in last]],
        halves,
        token,
        0,
        turn_beside,
        [in_hbm(left0), in_hbm(left0), up0, down0, up1, down1],
        tiles_from(2 * ROWS, 3 * ROWS, ROWS, ROWS, 6 * ROWS, 6 * ROWS),
        [in_hbm(array((4 * ROWS, CHIP))), array((4 * ROWS, CHIP))],
    )
    up3, down3 = move(up3, "y", 1), move(down3, "y", -1)
    (kept1, across1), token = turn(left1, up1, down1, up2, down2, token, 0, begun)
    (block,), token = tie([block], token, pltpu.HBM)
    across1 = move(across1, "xl", 1)
    (to_up, to_down), token = pass_on(left2, up2, down2, token)
    below2, above2 = move(to_up, "y", 1), move(to_down, "y", -1)
    (to_up, to_down), token = pass_on(left3, up3, down3, token)
    below3, above3 = move(to_up, "y", 1), move(to_down, "y", -1)
    (kept2, across2), token = turn(left2, up2, down2, below2, above2, token, keep=lambda a: a)
    across2 = move(across2, "xl", 1)
    (across1,), token = tie([across1], token)
    (kept3, across3), token = turn(left3, up3, down3, below3, above3, token, keep=lambda a: a)
    across3 = move(across3, "xl", 1)
    held, token = finish(places[:4], kept1, across1, block, (), token)
    held, token = finish(places[4:6], kept2, across2, block, held, token, lambda a: a)
    (out, sums), token = finish(places[6:], kept3, across3, block, held, token, lambda a: a)

    with jax.named_scope("bands"):
        sums = sums.reshape(8, 2, 8).transpose(1, 0, 2).reshape(2, 64)
        sums = sums + move(sums, "xh", 1)
        sums = (sums + move(sums, "z", 2)) + (move(sums, "z", 1) + move(sums, "z", -1))
    return out, sums * factor


def solution(mesh):
    fine = Mesh(mesh.devices.reshape(2, 4, 2, 4, 2), tuple(SIZES))
    row, col = ("xl", "y", "core"), ("z", "xh")
    return jax.shard_map(
        per_device,
        mesh=fine,
        in_specs=(P(None, row + col, None), P(row, col), P(row), P()),
        out_specs=(P(None, row, col), P(None, row)),
        check_vma=False,
    )
```
